256 devices in a mesh: ctx: 64 (over z, x, y_hi), kv: 4 (over y_lo, core).
Axes of the slice: x: 4, y: 4 (y_hi: 2, y_lo: 2; y = y_hi * 2 + y_lo), z: 8, core: 2. Of those that a mesh axis runs over, the one named last changes fastest.
Arguments:
- queries: bfloat16 [32, 16384], P(None, 'kv'), may hold values from -96 to 96
- cache_k: bfloat16 [524288, 1024], P('ctx', 'kv'), may hold values from -4 to 4
- cache_v: bfloat16 [524288, 1024], P('ctx', 'kv'), may hold values from -4 to 4
- kv_scale: float32 [2, 4096, 8], P(None, 'ctx', 'kv'), may hold values from 0.5 to 2
- new_kv: bfloat16 [2, 32, 1024], P(None, None, 'kv'), may hold values from -16 to 16
- fill_lengths: int32 [64], P('ctx'), may hold values from 1 to 8192, 393216 in all
- positions: int32 [32], replicated, may hold values from 0 to 31, each once
- out_weight: bfloat16 [16384, 16384], P('kv', 'ctx'), may hold values from -0.046875 to 0.046875
Outputs:
- projected: bfloat16 [32, 16384], P(None, 'ctx')
The draws below stay inside these ranges and needn't reach their ends.
All inputs are finite; a program needn't handle non-finite values. No bound on the sum of `fill_lengths` on one device may be relied on, other than what follows from the above.
Results may differ from the reference program's by a relative error of at most 0.027.
Values may be sent and summed in bfloat16 or wider, within the bound.
No kernel may reach another device: no remote copies, remote signals or barrier semaphores. Data moves between devices by JAX's collectives and lax.ppermute only.
A program may use at most 192 MiB of HBM per device.

```python
import math
import jax
import jax.numpy as jnp
import numpy as np
from jax import lax

H = 128
KVH = 8
DH = 128
DM = 16384
Q = 32
BLK = 128
CTX_DEV = 8192
CTX = 524288
N_CTX = 64
N_KV = 4


def draw_queries(key, part):
    key = jax.random.fold_in(key, 1)
    base = jnp.clip(jax.random.normal(key, (Q, H * DH), jnp.float32), -4.0, 4.0)
    return base.astype(jnp.bfloat16)


def draw_cache_k(key, part):
    key = jax.random.fold_in(key, 2)
    base = jnp.clip(jax.random.normal(key, (CTX, KVH * DH), jnp.float32), -4.0, 4.0)
    return base.astype(jnp.bfloat16)


def level_of(rng, extent, split, least, top_value):
    level, own = 1.0, jax.random.fold_in(rng, 6)
    for dim, blocks in split:
        draws = jnp.exp(jax.random.uniform(jax.random.fold_in(own, dim), (blocks,), jnp.float32, least / len(split), top_value / len(split)))
        level = level * jnp.repeat(draws, extent[dim] // blocks).reshape([-1 if axis == dim else 1 for axis in range(len(extent))])
    return level


def profile(count, total, most, slope):
    weights = [(1 << 20) // math.isqrt(grade ** slope) + 1 for grade in range(2, count + 1)]
    rest, given = total - most - (count - 1), [1] * (count - 1)
    while rest > 0:
        movable = [i for i in range(count - 1) if given[i] < most]
        whole, budget = sum([weights[i] for i in movable]), rest
        for i in movable:
            more = min(most - given[i], max(1, budget * weights[i] // whole), rest)
            given[i] = given[i] + more
            rest = rest - more
    return np.array([most] + given)


def uneven(key, count, total, bound, skew):
    if count == 2:
        one = jax.random.randint(key, (), max(1, total - bound), min(bound, total - 1) + 1)
        return jnp.stack([one, total - one])
    lengths = jnp.asarray(profile(count, total, bound, skew), jnp.int32)
    couples = (count - 1) // 2
    giver, receiver = lengths[1:1 + 2 * couples:2], lengths[2:2 + 2 * couples:2]
    slack = jnp.minimum(giver - 1, bound - receiver)
    moved = jax.random.randint(jax.random.fold_in(key, 1), (couples,), 0, 1 << 20) % (slack + 1)
    lengths = lengths.at[1:1 + 2 * couples:2].set(giver - moved).at[2:2 + 2 * couples:2].set(receiver + moved)
    return lengths[jax.random.permutation(jax.random.fold_in(key, 2), count)]


def normal_values(own_key, shape, width, limit, split=(), held_as=jnp.bfloat16):
    gain = level_of(own_key, shape, split, -0.22, 0.18) if split else 1.0
    entries = jax.random.normal(own_key, shape, jnp.float32) * width * gain
    return jnp.minimum(jnp.maximum(entries, -limit), limit).astype(held_as)


def setup_inputs(seed: int = 0) -> dict:
    key_list = jax.random.split(jax.random.key(seed), 9)
    return {
        "queries": draw_queries(jax.random.fold_in(key_list[8], 71), 0),
        "cache_k": draw_cache_k(jax.random.fold_in(key_list[8], 71), 0),
        "cache_v": normal_values(key_list[2], (CTX, KVH * DH), 1.0, 4.0, ((0, 64), (1, 4))),
        "kv_scale": jnp.clip(jnp.exp(math.log(2.0) - 1.3862944 * jax.random.uniform(key_list[3], (2, CTX // BLK, KVH), jnp.float32) ** level_of(key_list[3], (2, CTX // BLK, KVH), ((1, 64), (2, 4)), -0.2, 0.2)), 0.5, 2.0),
        "new_kv": normal_values(key_list[4], (2, Q, KVH * DH), 4.0, 16.0, ((2, 4),)),
        "fill_lengths": uneven(key_list[5], N_CTX, N_CTX * CTX_DEV * 3 // 4, CTX_DEV, 1).astype(jnp.int32),
        "positions": jax.random.permutation(key_list[6], Q).astype(jnp.int32),
        "out_weight": normal_values(key_list[7], (H * DH, DM), (H * DH) ** -0.5, 0.046875, ((0, 4), (1, 64))),
    }


def reference(queries, cache_k, cache_v, kv_scale, new_kv, fill_lengths, positions, out_weight):
    groups = H // KVH
    inv_root = 1.0 / math.sqrt(DH)
    query_f = queries.astype(jnp.float32).reshape(Q, KVH, groups, DH)
    scale_rows = jnp.repeat(kv_scale, BLK, axis=1).reshape(2, N_CTX, CTX_DEV, KVH)
    key_shards = cache_k.reshape(N_CTX, CTX_DEV, KVH, DH)
    value_shards = cache_v.reshape(N_CTX, CTX_DEV, KVH, DH)

    def visit_shard(state_in, shard_in):
        run_max, run_sum, run_num = state_in
        key_tile, value_tile, key_scale, value_scale, filled = shard_in
        raw_dot = jnp.einsum('qgsd,kgd->qgsk', query_f, key_tile.astype(jnp.float32))
        scores = raw_dot * key_scale.T[None, :, None, :] * inv_root
        visible = (jnp.arange(CTX_DEV, dtype=jnp.int32) < filled)[None, None, None, :]
        tile_max = lax.optimization_barrier(jnp.max(jnp.where(visible, scores, -1e+30), axis=-1))
        new_max = jnp.maximum(run_max, tile_max)
        weights_f = jnp.where(visible, jnp.exp(scores - new_max[..., None]), 0.0)
        weighted = (weights_f * value_scale.T[None, :, None, :]).astype(jnp.bfloat16)
        partial_num = jnp.einsum('qgsk,kgd->qgsd', weighted.astype(jnp.float32), value_tile.astype(jnp.float32))
        factor = jnp.exp(run_max - new_max)
        return ((new_max, run_sum * factor + lax.optimization_barrier(jnp.sum(weights_f, axis=-1)), run_num * factor[..., None] + partial_num), None)
    start = (jnp.full((Q, KVH, groups), -1e+30, jnp.float32), jnp.zeros((Q, KVH, groups), jnp.float32), jnp.zeros((Q, KVH, groups, DH), jnp.float32))
    (run_max, run_sum, run_num), _ = lax.scan(visit_shard, start, (key_shards, value_shards, scale_rows[0], scale_rows[1], fill_lengths.astype(jnp.int32)))
    new_keys = new_kv[0].astype(jnp.float32).reshape(Q, KVH, DH)
    new_values = new_kv[1].astype(jnp.float32).reshape(Q, KVH, DH)
    scores = jnp.einsum('qgsd,kgd->qgsk', query_f, new_keys) * inv_root
    visible = (positions[None, :] <= positions[:, None])[:, None, None, :]
    tile_max = lax.optimization_barrier(jnp.max(jnp.where(visible, scores, -1e+30), axis=-1))
    new_max = jnp.maximum(run_max, tile_max)
    weights_f = jnp.where(visible, jnp.exp(scores - new_max[..., None]), 0.0)
    partial_num = jnp.einsum('qgsk,kgd->qgsd', weights_f.astype(jnp.bfloat16).astype(jnp.float32), new_values)
    factor = jnp.exp(run_max - new_max)
    total = run_sum * factor + lax.optimization_barrier(jnp.sum(weights_f, axis=-1))
    numerator = run_num * factor[..., None] + partial_num
    attended = (numerator / total[..., None]).astype(jnp.bfloat16).reshape(Q, H * DH)
    rows_group = H * DH // N_KV
    attended_groups = attended.reshape(Q, N_KV, rows_group).transpose(1, 0, 2)
    weight_groups = out_weight.reshape(N_KV, rows_group, DM)

    def group_share(pair):
        left, right = pair
        return jnp.dot(left, right, preferred_element_type=jnp.float32).astype(jnp.bfloat16)
    shares = lax.map(group_share, (attended_groups, weight_groups))
    shares = lax.optimization_barrier(shares)
    return lax.optimization_barrier(jnp.sum(shares.astype(jnp.float32), axis=0)).astype(jnp.bfloat16)
```

```python
import functools
import math

import jax
import jax.numpy as jnp
from jax import lax
from jax.experimental import pallas as pl
from jax.experimental.pallas import tpu as pltpu
from jax.sharding import PartitionSpec as P

H = 128
KVH = 8
DH = 128
BLK = 128
GROUPS = H // KVH
HIDDEN = -1e30
TO_LOG2 = math.log2(math.e) / math.sqrt(DH)
NT = (((1,), (1,)), ((), ()))
NN = (((1,), (0,)), ((), ()))
F32 = jnp.float32
BF16 = jnp.bfloat16


def attend_kernel(tile_len, filled_ref, scale_ref, q_ref, k_ref, v_ref, out_ref, rows_ref, max_ref, acc_ref):
    t = pl.program_id(0)
    blocks = tile_len // BLK
    seen = filled_ref[0] - t * tile_len
    heads, rows, _ = rows_ref.shape
    qcount = q_ref.shape[0]

    @pl.when(t == 0)
    def _():
        for g in range(heads):
            for s in range(GROUPS):
                col = (g * GROUPS + s) * DH
                rows_ref[g, s * qcount : (s + 1) * qcount, :] = q_ref[:, col : col + DH]
        max_ref[...] = jnp.full_like(max_ref, HIDDEN)
        acc_ref[...] = jnp.zeros_like(acc_ref)

    def visit(masked):
        for g in range(heads):
            dots = lax.dot_general(
                rows_ref[g], k_ref[:, g * DH : (g + 1) * DH], NT, preferred_element_type=F32
            )
            scores, values = [], []
            for b in range(blocks):
                part = dots[:, b * BLK : (b + 1) * BLK] * (scale_ref[0, t * blocks + b, g] * TO_LOG2)
                if masked:
                    lane = lax.broadcasted_iota(jnp.int32, part.shape, 1)
                    part = jnp.where(lane < seen - b * BLK, part, HIDDEN)
                scores.append(part)
                value = v_ref[b * BLK : (b + 1) * BLK, g * DH : (g + 1) * DH].astype(F32)
                values.append((value * scale_ref[1, t * blocks + b, g]).astype(BF16))
            old_max = max_ref[g]
            tile_max = jnp.max(functools.reduce(jnp.maximum, scores), axis=1, keepdims=True)
            new_max = jnp.maximum(old_max, tile_max)
            max_ref[g] = new_max
            factor = jnp.exp2(old_max - new_max)
            weights = jnp.concatenate([jnp.exp2(x - new_max).astype(BF16) for x in scores], axis=1)
            value = jnp.concatenate(values, axis=0)
            value = jnp.concatenate([value, jnp.ones_like(value)], axis=1)
            part = lax.dot_general(weights, value, NN, preferred_element_type=F32)
            acc_ref[g] = acc_ref[g] * jnp.concatenate([factor, factor], axis=1) + part

    @pl.when(seen >= tile_len)
    def _():
        visit(False)

    @pl.when((seen > 0) & (seen < tile_len))
    def _():
        visit(True)

    @pl.when(t == pl.num_programs(0) - 1)
    def _():
        part = out_ref.shape[0] // heads
        for g in range(heads):
            top = max_ref[g].astype(BF16).astype(F32)
            factor = jnp.exp2(max_ref[g] - top)
            numer = (acc_ref[g, :, :DH] * factor).astype(BF16)
            total = acc_ref[g, :, DH:] * factor
            high = total.astype(BF16).astype(F32)
            lane = lax.broadcasted_iota(jnp.int32, total.shape, 1)
            stats = jnp.where(lane < 64, top, jnp.where(lane < 96, high, total - high)).astype(BF16)
            out_ref[g * part : (g + 1) * part, 0:16, :] = numer.reshape(part, 16, DH)
            out_ref[g * part : (g + 1) * part, 16:32, :] = stats.reshape(part, 16, DH)


def combine_kernel(place_ref, parts_ref, q_ref, new_ref, pos_row_ref, pos_col_ref, out_ref):
    place = place_ref[0]
    halves = q_ref.shape[0] // 16
    row = place % halves * 16
    column = place // halves * DH
    head = place // (halves * GROUPS) * DH
    q = q_ref[pl.ds(pl.multiple_of(row, 16), 16), pl.ds(pl.multiple_of(column, DH), DH)]
    new_keys = new_ref[0, :, pl.ds(pl.multiple_of(head, DH), DH)]
    new_values = new_ref[1, :, pl.ds(pl.multiple_of(head, DH), DH)]
    scores = lax.dot_general(q, new_keys, NT, preferred_element_type=F32) * TO_LOG2
    visible = pos_row_ref[...] <= pos_col_ref[pl.ds(pl.multiple_of(row, 16), 16), :]
    scores = jnp.where(visible, scores, HIDDEN)
    new_max = jnp.max(scores, axis=1, keepdims=True)

    stats = parts_ref[:, 16:32, :].astype(F32)
    tops = jnp.broadcast_to(stats[:, :, 0:1], stats.shape)
    totals = stats[:, :, 64:65] + stats[:, :, 96:97]
    top = jnp.maximum(jnp.max(tops, axis=0), new_max)
    factors = jnp.exp2(tops - top)
    weights = jnp.exp2(scores - top[:, 0:1])
    total = jnp.sum(totals * factors, axis=0) + jnp.sum(weights, axis=1, keepdims=True)
    numer = jnp.sum(parts_ref[:, 0:16, :].astype(F32) * factors, axis=0)
    numer = numer + lax.dot_general(
        weights.astype(BF16), new_values, NN, preferred_element_type=F32
    )
    attended = (numer / total).astype(BF16)
    out_ref[...] = jnp.broadcast_to(attended[None], out_ref.shape)


def project_kernel(parts_ref, weight_ref, out_ref, left_ref):
    qcount = left_ref.shape[0]
    halves = qcount // 16
    for i in range(parts_ref.shape[0]):
        row, col = i % halves * 16, i // halves * DH
        left_ref[row : row + 16, col : col + DH] = parts_ref[i]
    out_ref[...] = lax.dot_general(
        left_ref[...], weight_ref[...], NN, preferred_element_type=F32
    ).astype(BF16)


def per_device(queries, cache_k, cache_v, kv_scale, new_kv, fill_lengths, positions, out_weight):
    qcount, width = queries.shape
    heads = cache_k.shape[1] // DH
    shards = lax.axis_size("ctx")
    rows = qcount * GROUPS
    tile_len = 2048
    tiles = cache_k.shape[0] // tile_len
    smem = pl.BlockSpec(memory_space=pltpu.SMEM)
    vmem = pl.BlockSpec(memory_space=pltpu.VMEM)
    params = pltpu.CompilerParams(vmem_limit_bytes=48 * 1024 * 1024)

    parts = pl.pallas_call(
        functools.partial(attend_kernel, tile_len),
        grid=(tiles,),
        in_specs=[
            smem,
            smem,
            pl.BlockSpec((qcount, width), lambda t: (0, 0)),
            pl.BlockSpec((tile_len, heads * DH), lambda t: (t, 0)),
            pl.BlockSpec((tile_len, heads * DH), lambda t: (t, 0)),
        ],
        out_specs=pl.BlockSpec((shards, 32, DH), lambda t: (0, 0, 0)),
        out_shape=jax.ShapeDtypeStruct((shards, 32, DH), BF16),
        scratch_shapes=[
            pltpu.VMEM((heads, rows, DH), BF16),
            pltpu.VMEM((heads, rows, DH), F32),
            pltpu.VMEM((heads, rows, 2 * DH), F32),
        ],
        compiler_params=params,
        name="attend",
    )(fill_lengths, kv_scale, queries, cache_k, cache_v)

    parts = lax.all_to_all(parts, "ctx", 0, 0)

    attended = pl.pallas_call(
        combine_kernel,
        in_specs=[smem, vmem, vmem, vmem, vmem, vmem],
        out_specs=vmem,
        out_shape=jax.ShapeDtypeStruct((shards, 16, DH), BF16),
        compiler_params=params,
        name="combine",
    )(
        lax.axis_index("ctx").reshape(1),
        parts,
        queries,
        new_kv,
        positions.reshape(1, qcount),
        positions.reshape(qcount, 1),
    )

    attended = lax.all_to_all(attended, "ctx", 0, 0)

    share = pl.pallas_call(
        project_kernel,
        in_specs=[vmem, vmem],
        out_specs=vmem,
        out_shape=jax.ShapeDtypeStruct((qcount, out_weight.shape[1]), BF16),
        scratch_shapes=[pltpu.VMEM((qcount, width), BF16)],
        compiler_params=params,
        name="project",
    )(attended, out_weight)

    n = lax.axis_size("kv")
    total = share.astype(F32)
    for shift in range(1, n):
        other = lax.ppermute(share, "kv", [(i, (i + shift) % n) for i in range(n)])
        total = total + other.astype(F32)
    return total.astype(BF16)


def solution(mesh):
    placed = (
        P(None, "kv"),
        P("ctx", "kv"),
        P("ctx", "kv"),
        P(None, "ctx", "kv"),
        P(None, None, "kv"),
        P("ctx"),
        P(),
        P("kv", "ctx"),
    )
    return jax.shard_map(
        per_device, mesh=mesh, in_specs=placed, out_specs=P(None, "ctx"), check_vma=False
    )
```

```python
import functools
import math

import jax
import jax.numpy as jnp
from jax import lax
from jax.experimental import pallas as pl
from jax.experimental.pallas import tpu as pltpu
from jax.sharding import Mesh
from jax.sharding import PartitionSpec as P

H = 128
KVH = 8
DH = 128
BLK = 128
GROUPS = H // KVH
NEAR = 8
STATS = 16
HIDDEN = -1e30
LARGE = 2.0**100
TO_LOG2 = math.log2(math.e) / math.sqrt(DH)
NT = (((1,), (1,)), ((), ()))
NN = (((1,), (0,)), ((), ()))
F32 = jnp.float32
BF16 = jnp.bfloat16


def rounded(x):
    return x.astype(BF16).astype(F32)


def diagonal():
    row = lax.broadcasted_iota(jnp.int32, (DH, DH), 0)
    return row == lax.broadcasted_iota(jnp.int32, (DH, DH), 1)


def packed(top, total):
    high = rounded(total)
    row = lax.broadcasted_iota(jnp.int32, (STATS, DH), 0)
    return jnp.where(row == 0, top, jnp.where(row == 1, high, total - high)).astype(BF16)


def attend_kernel(
    tile_len, q_hbm, k_hbm, v_hbm, scale_hbm, filled_ref, out_ref,
    q_ref, k_ref, v_ref, scale_ref, k_sems, v_sems, sems, rows_ref, max_ref, acc_ref,
):
    blocks = tile_len // BLK
    heads, rows, _ = rows_ref.shape
    qcount = q_ref.shape[0]
    tiles = k_ref.shape[0] // tile_len
    chunks = 4
    size = rows // chunks

    def span(t):
        return pl.ds(t * tile_len, tile_len)

    def k_copy(t):
        return pltpu.make_async_copy(k_hbm.at[span(t)], k_ref.at[span(t)], k_sems.at[t])

    def v_copy(t):
        return pltpu.make_async_copy(v_hbm.at[span(t)], v_ref.at[span(t)], v_sems.at[t])

    small = [
        pltpu.make_async_copy(q_hbm, q_ref, sems.at[0]),
        pltpu.make_async_copy(scale_hbm, scale_ref, sems.at[1]),
    ]
    for copy in small:
        copy.start()
    for t in range(tiles):
        k_copy(t).start()
        v_copy(t).start()
    acc_ref[...] = jnp.zeros_like(acc_ref)
    for copy in small:
        copy.wait()
    for g in range(heads):
        for s in range(GROUPS):
            col = (g * GROUPS + s) * DH
            rows_ref[g, s * qcount : (s + 1) * qcount, :] = q_ref[:, col : col + DH]
    filled = filled_ref[0]

    def dots(t, g, c):
        return lax.dot_general(
            rows_ref[g, c * size : (c + 1) * size],
            k_ref[span(t), g * DH : (g + 1) * DH],
            NT,
            preferred_element_type=F32,
        )

    def scaled_values(t, g):
        values = []
        for b in range(blocks):
            value = v_ref[pl.ds(t * tile_len + b * BLK, BLK), g * DH : (g + 1) * DH].astype(F32)
            values.append((value * scale_ref[1, g, t * blocks + b]).astype(BF16))
        value = jnp.concatenate(values, axis=0)
        return jnp.concatenate([value, jnp.ones_like(value)], axis=1)

    def scores_of(t, g, dot, masked):
        scores = []
        for b in range(blocks):
            part = dot[:, b * BLK : (b + 1) * BLK] * (scale_ref[0, g, t * blocks + b] * TO_LOG2)
            if masked:
                lane = lax.broadcasted_iota(jnp.int32, part.shape, 1)
                part = jnp.where(lane < filled - t * tile_len - b * BLK, part, HIDDEN)
            scores.append(part)
        return scores

    def weigh(scores, top, value):
        weights = jnp.concatenate([jnp.exp2(x - top).astype(BF16) for x in scores], axis=1)
        return lax.dot_general(weights, value, NN, preferred_element_type=F32)

    def add(t, g, at, dot, value, masked):
        scores = scores_of(t, g, dot, masked)
        acc_ref[g, at] = acc_ref[g, at] + weigh(scores, max_ref[g, at], value)

    def add_rescaled(t, g, at, dot, value, masked):
        scores = scores_of(t, g, dot, masked)
        old_max = max_ref[g, at]
        tile_max = jnp.max(functools.reduce(jnp.maximum, scores), axis=1, keepdims=True)
        new_max = jnp.maximum(old_max, tile_max)
        max_ref[g, at] = new_max
        factor = jnp.exp2(old_max - new_max)
        factor = jnp.concatenate([factor, factor], axis=1)
        acc_ref[g, at] = acc_ref[g, at] * factor + weigh(scores, new_max, value)

    def visit(update, t, masked):
        items = [(g, c) for g in range(heads) for c in range(chunks)]
        dot = dots(t, *items[0])
        value = None
        for i, (g, c) in enumerate(items):
            following = dots(t, *items[i + 1]) if i + 1 < len(items) else None
            if c == 0:
                value = scaled_values(t, g)
            update(t, g, slice(c * size, (c + 1) * size), dot, value, masked)
            dot = following

    def visit_all(update, arrive):
        def step(t, carry):
            arrive(t)

            @pl.when(filled >= (t + 1) * tile_len)
            def _():
                visit(update, t, False)

            @pl.when((filled > t * tile_len) & (filled < (t + 1) * tile_len))
            def _():
                visit(update, t, True)

            return carry

        lax.fori_loop(0, tiles, step, 0)

    def arrive(t):
        @pl.when(t > 0)
        def _():
            k_copy(t).wait()

        v_copy(t).wait()

    k_copy(0).wait()
    for g in range(heads):
        first = lax.dot_general(
            rows_ref[g], k_ref[0:BLK, g * DH : (g + 1) * DH], NT, preferred_element_type=F32
        )
        first = first * (scale_ref[0, g, 0] * TO_LOG2)
        lane = lax.broadcasted_iota(jnp.int32, first.shape, 1)
        first = jnp.max(jnp.where(lane < filled, first, HIDDEN), axis=1, keepdims=True)
        max_ref[g] = jnp.broadcast_to(rounded(first), max_ref.shape[1:])
    visit_all(add, arrive)

    largest = jnp.max(acc_ref[:, :, DH:])

    @pl.when(jnp.logical_not(largest <= LARGE))
    def _():
        max_ref[...] = jnp.full_like(max_ref, HIDDEN)
        acc_ref[...] = jnp.zeros_like(acc_ref)
        visit_all(add_rescaled, lambda t: None)

    on_diagonal = diagonal()
    for i in range(out_ref.shape[0]):
        g, at = i * DH // rows, pl.ds(i * DH % rows, DH)
        top = rounded(max_ref[g, at])
        factor = jnp.exp2(max_ref[g, at] - top)
        out_ref[i, 0:DH, :] = (acc_ref[g, at, :DH] * factor).astype(BF16)
        total = jnp.where(on_diagonal, acc_ref[g, at, DH:] * factor, 0.0)
        top = jnp.where(on_diagonal, top, 0.0)
        out_ref[i, DH:, :] = packed(
            jnp.sum(top, axis=0, keepdims=True), jnp.sum(total, axis=0, keepdims=True)
        )


def merge(parts_ref, tops, totals, top):
    on_diagonal = diagonal()
    total = 0.0
    numer = 0.0
    for i, (one_top, one_total) in enumerate(zip(tops, totals)):
        factor = jnp.exp2(one_top - top)
        total = total + one_total * factor
        spread = jnp.where(on_diagonal, jnp.broadcast_to(factor, (DH, DH)), 0.0)
        high = spread.astype(BF16)
        low = (spread - high.astype(F32)).astype(BF16)
        part = parts_ref[i, 0:DH, :]
        numer = numer + lax.dot_general(high, part, NN, preferred_element_type=F32)
        numer = numer + lax.dot_general(low, part, NN, preferred_element_type=F32)
    return total, numer


def read_stats(parts_ref):
    tops, totals = [], []
    for i in range(parts_ref.shape[0]):
        stats = parts_ref[i, DH:, :].astype(F32)
        tops.append(stats[0:1])
        totals.append(stats[1:2] + stats[2:3])
    return tops, totals, functools.reduce(jnp.maximum, tops)


def merge_kernel(parts_ref, out_ref):
    tops, totals, top = read_stats(parts_ref)
    total, numer = merge(parts_ref, tops, totals, top)
    numer = numer.astype(BF16)
    stats = packed(top, total)
    for i in range(out_ref.shape[0]):
        out_ref[i, 0:DH, :] = numer
        out_ref[i, DH:, :] = stats


def finish_kernel(parts_ref, q_ref, new_ref, positions_ref, out_ref):
    place = lax.axis_index("near")
    qcount = q_ref.shape[0]
    groups = DH // qcount
    head = pl.multiple_of(place * groups // GROUPS * DH, DH)
    q = [
        q_ref[:, pl.ds(pl.multiple_of((place * groups + s) * DH, DH), DH)] for s in range(groups)
    ]
    q = jnp.concatenate(q, axis=0)
    new_keys = new_ref[0, :, pl.ds(head, DH)]
    new_values = new_ref[1, :, pl.ds(head, DH)]
    scores = lax.dot_general(q, new_keys, NT, preferred_element_type=F32) * TO_LOG2
    token = lax.broadcasted_iota(jnp.int32, scores.shape, 0) % qcount
    own = token == lax.broadcasted_iota(jnp.int32, scores.shape, 1)
    positions = jnp.broadcast_to(positions_ref[...], scores.shape)
    own_position = jnp.max(jnp.where(own, positions, -1), axis=1, keepdims=True)
    visible = positions <= own_position
    scores = jnp.where(visible, scores, HIDDEN)
    new_top = jnp.max(scores, axis=1, keepdims=True)
    on_diagonal = diagonal()

    def along_lanes(column):
        spread = jnp.where(on_diagonal, jnp.broadcast_to(column, (DH, DH)), 0.0)
        return jnp.sum(spread, axis=0, keepdims=True)

    def along_rows(row):
        spread = jnp.where(on_diagonal, jnp.broadcast_to(row, (DH, DH)), 0.0)
        return jnp.sum(spread, axis=1, keepdims=True)

    tops, totals, top = read_stats(parts_ref)
    top = jnp.maximum(top, along_lanes(new_top))
    total, numer = merge(parts_ref, tops, totals, top)
    weights = jnp.exp2(scores - along_rows(top))
    numer = numer + lax.dot_general(
        weights.astype(BF16), new_values, NN, preferred_element_type=F32
    )
    total = along_rows(total) + jnp.sum(weights, axis=1, keepdims=True)
    attended = (numer / total).astype(BF16)
    for i in range(out_ref.shape[0]):
        out_ref[i] = attended


def project_kernel(parts_ref, weight_ref, out_ref, left_ref):
    qcount = left_ref.shape[0]
    groups = DH // qcount
    for i in range(parts_ref.shape[0]):
        for s in range(groups):
            col = (i * groups + s) * DH
            left_ref[:, col : col + DH] = parts_ref[i, s * qcount : (s + 1) * qcount, :]
    out_ref[...] = lax.dot_general(
        left_ref[...], weight_ref[...], NN, preferred_element_type=F32
    ).astype(BF16)


def per_device(queries, cache_k, cache_v, kv_scale, new_kv, fill_lengths, positions, out_weight):
    qcount, width = queries.shape
    slots = cache_k.shape[0]
    heads = cache_k.shape[1] // DH
    rows = qcount * GROUPS
    near, far = lax.axis_size("near"), lax.axis_size("far")
    tile_len = 2048
    tiles = slots // tile_len
    smem = pl.BlockSpec(memory_space=pltpu.SMEM)
    vmem = pl.BlockSpec(memory_space=pltpu.VMEM)
    hbm = pl.BlockSpec(memory_space=pltpu.HBM)
    params = pltpu.CompilerParams(vmem_limit_bytes=48 * 1024 * 1024)

    def in_hbm(x):
        return pltpu.with_memory_space_constraint(x, pltpu.HBM)

    parts = pl.pallas_call(
        functools.partial(attend_kernel, tile_len),
        in_specs=[hbm, hbm, hbm, hbm, smem],
        out_specs=vmem,
        out_shape=jax.ShapeDtypeStruct((near, DH + STATS, DH), BF16),
        scratch_shapes=[
            pltpu.VMEM((qcount, width), BF16),
            pltpu.VMEM((slots, heads * DH), BF16),
            pltpu.VMEM((slots, heads * DH), BF16),
            pltpu.SMEM((2, heads, slots // BLK), F32),
            pltpu.SemaphoreType.DMA((tiles,)),
            pltpu.SemaphoreType.DMA((tiles,)),
            pltpu.SemaphoreType.DMA((2,)),
            pltpu.VMEM((heads, rows, DH), BF16),
            pltpu.VMEM((heads, rows, DH), F32),
            pltpu.VMEM((heads, rows, 2 * DH), F32),
        ],
        compiler_params=params,
        name="attend",
    )(
        in_hbm(queries),
        in_hbm(cache_k),
        in_hbm(cache_v),
        in_hbm(kv_scale.transpose(0, 2, 1)),
        fill_lengths,
    )

    parts = lax.all_to_all(parts, "near", 0, 0)
    parts = pl.pallas_call(
        merge_kernel,
        in_specs=[vmem],
        out_specs=vmem,
        out_shape=jax.ShapeDtypeStruct((far, DH + STATS, DH), BF16),
        compiler_params=params,
        name="merge",
    )(parts)
    parts = lax.all_to_all(parts, "far", 0, 0)

    attended = pl.pallas_call(
        finish_kernel,
        in_specs=[vmem, vmem, vmem, vmem],
        out_specs=vmem,
        out_shape=jax.ShapeDtypeStruct((near, DH, DH), BF16),
        compiler_params=params,
        name="finish",
    )(
        parts,
        queries,
        new_kv,
        positions.reshape(1, qcount),
    )
    attended = lax.all_to_all(attended, "near", 0, 0)

    share = pl.pallas_call(
        project_kernel,
        in_specs=[vmem, vmem],
        out_specs=vmem,
        out_shape=jax.ShapeDtypeStruct((qcount, out_weight.shape[1]), BF16),
        scratch_shapes=[pltpu.VMEM((qcount, width), BF16)],
        compiler_params=params,
        name="project",
    )(attended, out_weight)

    n = lax.axis_size("kv")
    total = share.astype(F32)
    for shift in range(1, n):
        other = lax.ppermute(share, "kv", [(i, (i + shift) % n) for i in range(n)])
        total = total + other.astype(F32)
    return total.astype(BF16)


def solution(mesh):
    ctx, kv = mesh.devices.shape
    mesh = Mesh(mesh.devices.reshape(ctx // NEAR, NEAR, kv), ("far", "near", "kv"))
    ctx = ("far", "near")
    placed = (
        P(None, "kv"),
        P(ctx, "kv"),
        P(ctx, "kv"),
        P(None, ctx, "kv"),
        P(None, None, "kv"),
        P(ctx),
        P(),
        P("kv", ctx),
    )
    return jax.shard_map(
        per_device, mesh=mesh, in_specs=placed, out_specs=P(None, ctx), check_vma=False
    )
```

```python
import functools
import math

import jax
import jax.numpy as jnp
from jax import lax
from jax.experimental import pallas as pl
from jax.experimental.pallas import tpu as pltpu
from jax.sharding import Mesh
from jax.sharding import PartitionSpec as P

H = 128
KVH = 8
DH = 128
BLK = 128
GROUPS = H // KVH
NEAR = 8
STATS = 16
EARLY = 512
COUNT = 16
PIECE = 256
WIDTH = 256
HIDDEN = -1e30
LARGE = 2.0**100
TO_LOG2 = math.log2(math.e) / math.sqrt(DH)
NT = (((1,), (1,)), ((), ()))
NN = (((1,), (0,)), ((), ()))
F32 = jnp.float32
BF16 = jnp.bfloat16


def rounded(x):
    return x.astype(BF16).astype(F32)


def diagonal():
    row = lax.broadcasted_iota(jnp.int32, (DH, DH), 0)
    return row == lax.broadcasted_iota(jnp.int32, (DH, DH), 1)


def packed(top, total):
    high = rounded(total)
    row = lax.broadcasted_iota(jnp.int32, (STATS, DH), 0)
    return jnp.where(row == 0, top, jnp.where(row == 1, high, total - high)).astype(BF16)


def attend_kernel(
    tile_len, q_hbm, k_hbm, v_hbm, scale_hbm, filled_ref, out_ref,
    q_ref, k_ref, v_ref, scale_ref, k_sems, v_sems, sems, rows_ref, max_ref, acc_ref, even_ref, odd_ref,
):
    blocks = tile_len // BLK
    heads, rows, _ = rows_ref.shape
    qcount = q_ref.shape[0]
    tiles = k_ref.shape[0] // tile_len
    size = WIDTH
    chunks = rows // size

    def span(t):
        return pl.ds(t * tile_len, tile_len)

    def k_copy(t):
        return pltpu.make_async_copy(k_hbm.at[span(t)], k_ref.at[span(t)], k_sems.at[t])

    def v_copy(t):
        return pltpu.make_async_copy(v_hbm.at[span(t)], v_ref.at[span(t)], v_sems.at[t])

    small = [
        pltpu.make_async_copy(q_hbm, q_ref, sems.at[0]),
        pltpu.make_async_copy(scale_hbm, scale_ref, sems.at[1]),
    ]
    for copy in small:
        copy.start()
    early = pl.ds(0, EARLY)
    late = pl.ds(EARLY, tile_len - EARLY)
    k_early = pltpu.make_async_copy(k_hbm.at[early], k_ref.at[early], sems.at[2])
    k_late = pltpu.make_async_copy(k_hbm.at[late], k_ref.at[late], k_sems.at[0])
    k_early.start()
    k_late.start()
    v_copy(0).start()
    acc_ref[...] = jnp.zeros_like(acc_ref)
    for copy in small:
        copy.wait()
    for g in range(heads):
        for s in range(GROUPS):
            col = (g * GROUPS + s) * DH
            rows_ref[g, s * qcount : (s + 1) * qcount, :] = q_ref[:, col : col + DH]
    filled = filled_ref[0]

    def scores_of(t, g, at, p, masked):
        start = t * tile_len + p * PIECE
        dot = lax.dot_general(
            k_ref[pl.ds(start, PIECE), g * DH : (g + 1) * DH],
            rows_ref[g, at],
            NT,
            preferred_element_type=F32,
        )
        scores = []
        for i in range(PIECE // BLK):
            scale = scale_ref[0, g, t * blocks + p * (PIECE // BLK) + i] * TO_LOG2
            part = dot[i * BLK : (i + 1) * BLK] * scale
            if masked:
                slot = lax.broadcasted_iota(jnp.int32, part.shape, 0)
                part = jnp.where(slot < filled - start - i * BLK, part, HIDDEN)
            scores.append(part)
        return scores

    def scaled_values(t, g):
        values = []
        for b in range(blocks):
            value = v_ref[pl.ds(t * tile_len + b * BLK, BLK), g * DH : (g + 1) * DH].astype(F32)
            values.append((value * scale_ref[1, g, t * blocks + b]).astype(BF16).T)
        value = jnp.concatenate(values, axis=1)
        return jnp.concatenate([value, jnp.ones((COUNT, tile_len), BF16)], axis=0)

    pieces = range(tile_len // PIECE)

    def weigh_rescaled(t, g, at, masked):
        scores = []
        for p in pieces:
            scores += scores_of(t, g, at, p, masked)
        old_max = max_ref[g, :, at]
        tile_max = jnp.max(functools.reduce(jnp.maximum, scores), axis=0, keepdims=True)
        new_max = jnp.maximum(old_max, tile_max)
        max_ref[g, :, at] = new_max
        weights = jnp.concatenate([jnp.exp2(x - new_max).astype(BF16) for x in scores], axis=0)
        return weights, jnp.exp2(old_max - new_max)

    def visit(weigh, t, masked):
        items = [(g, slice(c * size, (c + 1) * size)) for g in range(heads) for c in range(chunks)]
        held = weigh(t, *items[0], masked)
        values = {}
        for i, (g, at) in enumerate(items):
            following = weigh(t, *items[i + 1], masked) if i + 1 < len(items) else None
            if g not in values:
                values[g] = scaled_values(t, g)
            weights, factor = held
            part = lax.dot_general(values[g], weights, NN, preferred_element_type=F32)
            before = acc_ref[g, :, at]
            acc_ref[g, :, at] = (before if factor is None else before * factor) + part
            held = following

    def visit_all():
        def step(t, carry):
            @pl.when(filled >= (t + 1) * tile_len)
            def _():
                visit(weigh_rescaled, t, False)

            @pl.when((filled > t * tile_len) & (filled < (t + 1) * tile_len))
            def _():
                visit(weigh_rescaled, t, True)

            return carry

        lax.fori_loop(0, tiles, step, 0)

    def fill_weights(weights_ref, t, g, masked=False):
        for p in pieces:
            scores = scores_of(t, g, slice(None), p, masked)
            for i, x in enumerate(scores):
                row = p * PIECE + i * BLK
                weights_ref[g, row : row + BLK, :] = jnp.exp2(x - max_ref[g]).astype(BF16)

    def use_weights(weights_ref, t, g):
        part = lax.dot_general(
            scaled_values(t, g), weights_ref[g], NN, preferred_element_type=F32
        )
        acc_ref[g] = acc_ref[g] + part

    def both(fill_ref, following, use_ref, t):
        k_copy(following).wait()
        v_copy(t).wait()
        for g in range(heads):
            fill_weights(fill_ref, following, g)
            use_weights(use_ref, t, g)

    def visit_once():
        full = filled // tile_len

        @pl.when(full > 0)
        def _():
            for g in range(heads):
                fill_weights(even_ref, 0, g)

        def pair(i, carry):
            both(odd_ref, 2 * i + 1, even_ref, 2 * i)
            both(even_ref, 2 * i + 2, odd_ref, 2 * i + 1)
            return carry

        pairs = (full - 1) // 2
        lax.fori_loop(0, pairs, pair, 0)
        last = 2 * pairs

        @pl.when((full > 0) & (full % 2 == 1))
        def _():
            v_copy(last).wait()
            for g in range(heads):
                use_weights(even_ref, last, g)

        @pl.when((full > 0) & (full % 2 == 0))
        def _():
            both(odd_ref, last + 1, even_ref, last)
            v_copy(last + 1).wait()
            for g in range(heads):
                use_weights(odd_ref, last + 1, g)

        def skip(t, carry):
            @pl.when(t > 0)
            def _():
                k_copy(t).wait()

            v_copy(t).wait()
            return carry

        lax.fori_loop(full, tiles, skip, 0)

        @pl.when(full * tile_len < filled)
        def _():
            for g in range(heads):
                fill_weights(even_ref, full, g, True)
                use_weights(even_ref, full, g)

    k_early.wait()
    for g in range(heads):
        first = lax.dot_general(
            k_ref[0:BLK, g * DH : (g + 1) * DH], rows_ref[g], NT, preferred_element_type=F32
        )
        first = first * (scale_ref[0, g, 0] * TO_LOG2)
        slot = lax.broadcasted_iota(jnp.int32, first.shape, 0)
        first = jnp.max(jnp.where(slot < filled, first, HIDDEN), axis=0, keepdims=True)
        max_ref[g] = rounded(first)
    k_late.wait()
    for t in range(1, tiles):
        k_copy(t).start()
        v_copy(t).start()
    visit_once()

    largest = jnp.max(acc_ref[:, DH:, :])

    @pl.when(jnp.logical_not(largest <= LARGE))
    def _():
        max_ref[...] = jnp.full_like(max_ref, HIDDEN)
        acc_ref[...] = jnp.zeros_like(acc_ref)
        visit_all()

    for i in range(out_ref.shape[0]):
        g, at = i * DH // rows, pl.ds(i * DH % rows, DH)
        top = rounded(max_ref[g, :, at])
        factor = jnp.exp2(max_ref[g, :, at] - top)
        out_ref[i, 0:DH, :] = (acc_ref[g, 0:DH, at] * factor).T.astype(BF16)
        out_ref[i, DH:, :] = packed(top, acc_ref[g, DH : DH + 1, at] * factor)


def attend_scratch(qcount, width, slots, heads, tile_len):
    rows = qcount * GROUPS
    tiles = slots // tile_len
    return [
        pltpu.VMEM((qcount, width), BF16),
        pltpu.VMEM((slots, heads * DH), BF16),
        pltpu.VMEM((slots, heads * DH), BF16),
        pltpu.SMEM((2, heads, slots // BLK), F32),
        pltpu.SemaphoreType.DMA((tiles,)),
        pltpu.SemaphoreType.DMA((tiles,)),
        pltpu.SemaphoreType.DMA((3,)),
        pltpu.VMEM((heads, rows, DH), BF16),
        pltpu.VMEM((heads, 1, rows), F32),
        pltpu.VMEM((heads, DH + COUNT, rows), F32),
        pltpu.VMEM((heads, tile_len, rows), BF16),
        pltpu.VMEM((heads, tile_len, rows), BF16),
    ]


def merge(parts_ref, tops, totals, top):
    on_diagonal = diagonal()
    total = 0.0
    numer = 0.0
    for i, (one_top, one_total) in enumerate(zip(tops, totals)):
        factor = jnp.exp2(one_top - top)
        total = total + one_total * factor
        spread = jnp.where(on_diagonal, jnp.broadcast_to(factor, (DH, DH)), 0.0)
        high = spread.astype(BF16)
        low = (spread - high.astype(F32)).astype(BF16)
        part = parts_ref[i, 0:DH, :]
        numer = numer + lax.dot_general(high, part, NN, preferred_element_type=F32)
        numer = numer + lax.dot_general(low, part, NN, preferred_element_type=F32)
    return total, numer


def read_stats(parts_ref):
    tops, totals = [], []
    for i in range(parts_ref.shape[0]):
        stats = parts_ref[i, DH:, :].astype(F32)
        tops.append(stats[0:1])
        totals.append(stats[1:2] + stats[2:3])
    return tops, totals, functools.reduce(jnp.maximum, tops)


def merge_kernel(parts_ref, out_ref):
    tops, totals, top = read_stats(parts_ref)
    total, numer = merge(parts_ref, tops, totals, top)
    numer = numer.astype(BF16)
    stats = packed(top, total)
    for i in range(out_ref.shape[0]):
        out_ref[i, 0:DH, :] = numer
        out_ref[i, DH:, :] = stats


def finish_kernel(parts_ref, q_ref, new_ref, positions_ref, out_ref):
    place = lax.axis_index("near")
    qcount = q_ref.shape[0]
    groups = DH // qcount
    head = pl.multiple_of(place * groups // GROUPS * DH, DH)
    q = [
        q_ref[:, pl.ds(pl.multiple_of((place * groups + s) * DH, DH), DH)] for s in range(groups)
    ]
    q = jnp.concatenate(q, axis=0)
    new_keys = new_ref[0, :, pl.ds(head, DH)]
    new_values = new_ref[1, :, pl.ds(head, DH)]
    scores = lax.dot_general(q, new_keys, NT, preferred_element_type=F32) * TO_LOG2
    token = lax.broadcasted_iota(jnp.int32, scores.shape, 0) % qcount
    own = token == lax.broadcasted_iota(jnp.int32, scores.shape, 1)
    positions = jnp.broadcast_to(positions_ref[...], scores.shape)
    own_position = jnp.max(jnp.where(own, positions, -1), axis=1, keepdims=True)
    visible = positions <= own_position
    scores = jnp.where(visible, scores, HIDDEN)
    new_top = jnp.max(scores, axis=1, keepdims=True)
    on_diagonal = diagonal()

    def along_lanes(column):
        spread = jnp.where(on_diagonal, jnp.broadcast_to(column, (DH, DH)), 0.0)
        return jnp.sum(spread, axis=0, keepdims=True)

    def along_rows(row):
        spread = jnp.where(on_diagonal, jnp.broadcast_to(row, (DH, DH)), 0.0)
        return jnp.sum(spread, axis=1, keepdims=True)

    tops, totals, top = read_stats(parts_ref)
    top = jnp.maximum(top, along_lanes(new_top))
    total, numer = merge(parts_ref, tops, totals, top)
    weights = jnp.exp2(scores - along_rows(top))
    numer = numer + lax.dot_general(
        weights.astype(BF16), new_values, NN, preferred_element_type=F32
    )
    total = along_rows(total) + jnp.sum(weights, axis=1, keepdims=True)
    attended = (numer / total).astype(BF16)
    for i in range(out_ref.shape[0]):
        out_ref[i] = attended


def project_kernel(parts_ref, weight_ref, out_ref, left_ref):
    qcount = left_ref.shape[0]
    groups = DH // qcount
    for i in range(parts_ref.shape[0]):
        for s in range(groups):
            col = (i * groups + s) * DH
            left_ref[:, col : col + DH] = parts_ref[i, s * qcount : (s + 1) * qcount, :]
    out_ref[...] = lax.dot_general(
        left_ref[...], weight_ref[...], NN, preferred_element_type=F32
    ).astype(BF16)


def per_device(queries, cache_k, cache_v, kv_scale, new_kv, fill_lengths, positions, out_weight):
    qcount, width = queries.shape
    slots = cache_k.shape[0]
    heads = cache_k.shape[1] // DH
    near, far = lax.axis_size("near"), lax.axis_size("far")
    tile_len = 2048
    smem = pl.BlockSpec(memory_space=pltpu.SMEM)
    vmem = pl.BlockSpec(memory_space=pltpu.VMEM)
    hbm = pl.BlockSpec(memory_space=pltpu.HBM)
    params = pltpu.CompilerParams(vmem_limit_bytes=48 * 1024 * 1024)

    def in_hbm(x):
        return pltpu.with_memory_space_constraint(x, pltpu.HBM)

    parts = pl.pallas_call(
        functools.partial(attend_kernel, tile_len),
        in_specs=[hbm, hbm, hbm, hbm, smem],
        out_specs=vmem,
        out_shape=jax.ShapeDtypeStruct((near, DH + STATS, DH), BF16),
        scratch_shapes=attend_scratch(qcount, width, slots, heads, tile_len),
        compiler_params=params,
        name="attend",
    )(
        in_hbm(queries),
        in_hbm(cache_k),
        in_hbm(cache_v),
        in_hbm(kv_scale.transpose(0, 2, 1)),
        fill_lengths,
    )

    parts = lax.all_to_all(parts, "near", 0, 0)
    parts = pl.pallas_call(
        merge_kernel,
        in_specs=[vmem],
        out_specs=vmem,
        out_shape=jax.ShapeDtypeStruct((far, DH + STATS, DH), BF16),
        compiler_params=params,
        name="merge",
    )(parts)
    parts = lax.all_to_all(parts, "far", 0, 0)

    attended = pl.pallas_call(
        finish_kernel,
        in_specs=[vmem, vmem, vmem, vmem],
        out_specs=vmem,
        out_shape=jax.ShapeDtypeStruct((near, DH, DH), BF16),
        compiler_params=params,
        name="finish",
    )(
        parts,
        queries,
        new_kv,
        positions.reshape(1, qcount),
    )
    attended = lax.all_to_all(attended, "near", 0, 0)

    share = pl.pallas_call(
        project_kernel,
        in_specs=[vmem, vmem],
        out_specs=vmem,
        out_shape=jax.ShapeDtypeStruct((qcount, out_weight.shape[1]), BF16),
        scratch_shapes=[pltpu.VMEM((qcount, width), BF16)],
        compiler_params=params,
        name="project",
    )(attended, out_weight)

    n = lax.axis_size("kv")
    total = share.astype(F32)
    for shift in range(1, n):
        other = lax.ppermute(share, "kv", [(i, (i + shift) % n) for i in range(n)])
        total = total + other.astype(F32)
    return total.astype(BF16)


def solution(mesh):
    ctx, kv = mesh.devices.shape
    mesh = Mesh(mesh.devices.reshape(ctx // NEAR, NEAR, kv), ("far", "near", "kv"))
    ctx = ("far", "near")
    placed = (
        P(None, "kv"),
        P(ctx, "kv"),
        P(ctx, "kv"),
        P(None, ctx, "kv"),
        P(None, None, "kv"),
        P(ctx),
        P(),
        P("kv", ctx),
    )
    return jax.shard_map(
        per_device, mesh=mesh, in_specs=placed, out_specs=P(None, ctx), check_vma=False
    )
```

```python
import functools
import math

import jax
import jax.numpy as jnp
from jax import lax
from jax.experimental import pallas as pl
from jax.experimental.pallas import tpu as pltpu
from jax.sharding import Mesh
from jax.sharding import PartitionSpec as P

H = 128
KVH = 8
DH = 128
BLK = 128
GROUPS = H // KVH
NEAR = 8
STATS = 16
EARLY = 512
COUNT = 16
PIECE = 256
WIDTH = 256
HIDDEN = -1e30
LARGE = 2.0**100
TO_LOG2 = math.log2(math.e) / math.sqrt(DH)
NT = (((1,), (1,)), ((), ()))
NN = (((1,), (0,)), ((), ()))
F32 = jnp.float32
BF16 = jnp.bfloat16


def rounded(x):
    return x.astype(BF16).astype(F32)


def diagonal():
    row = lax.broadcasted_iota(jnp.int32, (DH, DH), 0)
    return row == lax.broadcasted_iota(jnp.int32, (DH, DH), 1)


def packed(top, total):
    high = rounded(total)
    row = lax.broadcasted_iota(jnp.int32, (STATS, DH), 0)
    return jnp.where(row == 0, top, jnp.where(row == 1, high, total - high)).astype(BF16)


def attend_kernel(
    tile_len, q_hbm, k_hbm, v_hbm, scale_hbm, filled_ref, out_ref,
    q_ref, k_ref, v_ref, scale_ref, k_sems, v_sems, sems, rows_ref, max_ref, acc_ref, even_ref, odd_ref,
):
    blocks = tile_len // BLK
    heads, rows, _ = rows_ref.shape
    qcount = q_ref.shape[0]
    tiles = k_ref.shape[0] // tile_len
    size = WIDTH
    chunks = rows // size

    def span(t):
        return pl.ds(t * tile_len, tile_len)

    def k_copy(t):
        return pltpu.make_async_copy(k_hbm.at[span(t)], k_ref.at[span(t)], k_sems.at[t])

    def v_copy(t):
        return pltpu.make_async_copy(v_hbm.at[span(t)], v_ref.at[span(t)], v_sems.at[t])

    small = [
        pltpu.make_async_copy(q_hbm, q_ref, sems.at[0]),
        pltpu.make_async_copy(scale_hbm, scale_ref, sems.at[1]),
    ]
    for copy in small:
        copy.start()
    early = pl.ds(0, EARLY)
    late = pl.ds(EARLY, tile_len - EARLY)
    k_early = pltpu.make_async_copy(k_hbm.at[early], k_ref.at[early], sems.at[2])
    k_late = pltpu.make_async_copy(k_hbm.at[late], k_ref.at[late], k_sems.at[0])
    k_early.start()
    k_late.start()
    v_copy(0).start()
    acc_ref[...] = jnp.zeros_like(acc_ref)
    for copy in small:
        copy.wait()
    for g in range(heads):
        for s in range(GROUPS):
            col = (g * GROUPS + s) * DH
            rows_ref[g, s * qcount : (s + 1) * qcount, :] = q_ref[:, col : col + DH]
    filled = filled_ref[0]

    def scores_of(t, g, at, p, masked):
        start = t * tile_len + p * PIECE
        dot = lax.dot_general(
            k_ref[pl.ds(start, PIECE), g * DH : (g + 1) * DH],
            rows_ref[g, at],
            NT,
            preferred_element_type=F32,
        )
        scores = []
        for i in range(PIECE // BLK):
            scale = scale_ref[0, g, t * blocks + p * (PIECE // BLK) + i] * TO_LOG2
            part = dot[i * BLK : (i + 1) * BLK] * scale
            if masked:
                slot = lax.broadcasted_iota(jnp.int32, part.shape, 0)
                part = jnp.where(slot < filled - start - i * BLK, part, HIDDEN)
            scores.append(part)
        return scores

    def scaled_values(t, g):
        values = []
        for b in range(blocks):
            value = v_ref[pl.ds(t * tile_len + b * BLK, BLK), g * DH : (g + 1) * DH].astype(F32)
            values.append((value * scale_ref[1, g, t * blocks + b]).astype(BF16).T)
        value = jnp.concatenate(values, axis=1)
        return jnp.concatenate([value, jnp.ones((COUNT, tile_len), BF16)], axis=0)

    pieces = range(tile_len // PIECE)

    def weigh_rescaled(t, g, at, masked):
        scores = []
        for p in pieces:
            scores += scores_of(t, g, at, p, masked)
        old_max = max_ref[g, :, at]
        tile_max = jnp.max(functools.reduce(jnp.maximum, scores), axis=0, keepdims=True)
        new_max = jnp.maximum(old_max, tile_max)
        max_ref[g, :, at] = new_max
        weights = jnp.concatenate([jnp.exp2(x - new_max).astype(BF16) for x in scores], axis=0)
        return weights, jnp.exp2(old_max - new_max)

    def visit(weigh, t, masked):
        items = [(g, slice(c * size, (c + 1) * size)) for g in range(heads) for c in range(chunks)]
        held = weigh(t, *items[0], masked)
        values = {}
        for i, (g, at) in enumerate(items):
            following = weigh(t, *items[i + 1], masked) if i + 1 < len(items) else None
            if g not in values:
                values[g] = scaled_values(t, g)
            weights, factor = held
            part = lax.dot_general(values[g], weights, NN, preferred_element_type=F32)
            before = acc_ref[g, :, at]
            acc_ref[g, :, at] = (before if factor is None else before * factor) + part
            held = following

    def visit_all():
        def step(t, carry):
            @pl.when(filled >= (t + 1) * tile_len)
            def _():
                visit(weigh_rescaled, t, False)

            @pl.when((filled > t * tile_len) & (filled < (t + 1) * tile_len))
            def _():
                visit(weigh_rescaled, t, True)

            return carry

        lax.fori_loop(0, tiles, step, 0)

    def fill_weights(weights_ref, t, g, masked=False):
        for p in pieces:
            scores = scores_of(t, g, slice(None), p, masked)
            for i, x in enumerate(scores):
                row = p * PIECE + i * BLK
                weights_ref[g, row : row + BLK, :] = jnp.exp2(x - max_ref[g]).astype(BF16)

    def use_weights(weights_ref, t, g):
        part = lax.dot_general(
            scaled_values(t, g), weights_ref[g], NN, preferred_element_type=F32
        )
        acc_ref[g] = acc_ref[g] + part

    def both(fill_ref, following, use_ref, t, wait=True):
        if wait:
            k_copy(following).wait()
            v_copy(t).wait()
        for g in range(heads):
            fill_weights(fill_ref, following, g)
            use_weights(use_ref, t, g)

    def visit_once():
        full = filled // tile_len

        @pl.when(full > 0)
        def _():
            for g in range(heads):
                fill_weights(even_ref, 0, g)

        def pair(i, carry):
            both(odd_ref, 2 * i + 1, even_ref, 2 * i)
            both(even_ref, 2 * i + 2, odd_ref, 2 * i + 1)
            return carry

        pairs = (full - 1) // 2
        lax.fori_loop(0, pairs, pair, 0)
        last = 2 * pairs

        @pl.when((full > 0) & (full % 2 == 1))
        def _():
            v_copy(last).wait()
            for g in range(heads):
                use_weights(even_ref, last, g)

        @pl.when((full > 0) & (full % 2 == 0))
        def _():
            both(odd_ref, last + 1, even_ref, last)
            v_copy(last + 1).wait()
            for g in range(heads):
                use_weights(odd_ref, last + 1, g)

        def skip(t, carry):
            @pl.when(t > 0)
            def _():
                k_copy(t).wait()

            v_copy(t).wait()
            return carry

        lax.fori_loop(full, tiles, skip, 0)

        @pl.when(full * tile_len < filled)
        def _():
            for g in range(heads):
                fill_weights(even_ref, full, g, True)
                use_weights(even_ref, full, g)

    k_early.wait()
    for g in range(heads):
        first = lax.dot_general(
            k_ref[0:BLK, g * DH : (g + 1) * DH], rows_ref[g], NT, preferred_element_type=F32
        )
        first = first * (scale_ref[0, g, 0] * TO_LOG2)
        slot = lax.broadcasted_iota(jnp.int32, first.shape, 0)
        first = jnp.max(jnp.where(slot < filled, first, HIDDEN), axis=0, keepdims=True)
        max_ref[g] = rounded(first)
    k_late.wait()
    for t in range(1, tiles):
        k_copy(t).start()
        v_copy(t).start()

    @pl.when(filled >= tiles * tile_len)
    def _():
        held = [even_ref, odd_ref]
        for g in range(heads):
            fill_weights(even_ref, 0, g)
        both(odd_ref, 1, even_ref, 0)
        for t in range(2, tiles):
            k_copy(t).wait()
        for t in range(1, tiles):
            v_copy(t).wait()
        for t in range(2, tiles):
            both(held[t % 2], t, held[1 - t % 2], t - 1, False)
        for g in range(heads):
            use_weights(held[(tiles - 1) % 2], tiles - 1, g)

    @pl.when(filled < tiles * tile_len)
    def _():
        visit_once()

    largest = jnp.max(acc_ref[:, DH:, :])

    @pl.when(jnp.logical_not(largest <= LARGE))
    def _():
        max_ref[...] = jnp.full_like(max_ref, HIDDEN)
        acc_ref[...] = jnp.zeros_like(acc_ref)
        visit_all()

    for i in range(out_ref.shape[0]):
        g, at = i * DH // rows, pl.ds(i * DH % rows, DH)
        top = rounded(max_ref[g, :, at])
        factor = jnp.exp2(max_ref[g, :, at] - top)
        out_ref[i, 0:DH, :] = (acc_ref[g, 0:DH, at] * factor).T.astype(BF16)
        out_ref[i, DH:, :] = packed(top, acc_ref[g, DH : DH + 1, at] * factor)


def attend_scratch(qcount, width, slots, heads, tile_len):
    rows = qcount * GROUPS
    tiles = slots // tile_len
    return [
        pltpu.VMEM((qcount, width), BF16),
        pltpu.VMEM((slots, heads * DH), BF16),
        pltpu.VMEM((slots, heads * DH), BF16),
        pltpu.SMEM((2, heads, slots // BLK), F32),
        pltpu.SemaphoreType.DMA((tiles,)),
        pltpu.SemaphoreType.DMA((tiles,)),
        pltpu.SemaphoreType.DMA((3,)),
        pltpu.VMEM((heads, rows, DH), BF16),
        pltpu.VMEM((heads, 1, rows), F32),
        pltpu.VMEM((heads, DH + COUNT, rows), F32),
        pltpu.VMEM((heads, tile_len, rows), BF16),
        pltpu.VMEM((heads, tile_len, rows), BF16),
    ]


def merge(parts_ref, tops, totals, top):
    on_diagonal = diagonal()
    total = 0.0
    numer = 0.0
    for i, (one_top, one_total) in enumerate(zip(tops, totals)):
        factor = jnp.exp2(one_top - top)
        total = total + one_total * factor
        spread = jnp.where(on_diagonal, jnp.broadcast_to(factor, (DH, DH)), 0.0)
        high = spread.astype(BF16)
        low = (spread - high.astype(F32)).astype(BF16)
        part = parts_ref[i, 0:DH, :]
        numer = numer + lax.dot_general(high, part, NN, preferred_element_type=F32)
        numer = numer + lax.dot_general(low, part, NN, preferred_element_type=F32)
    return total, numer


def read_stats(parts_ref):
    tops, totals = [], []
    for i in range(parts_ref.shape[0]):
        stats = parts_ref[i, DH:, :].astype(F32)
        tops.append(stats[0:1])
        totals.append(stats[1:2] + stats[2:3])
    return tops, totals, functools.reduce(jnp.maximum, tops)


def merge_kernel(parts_ref, out_ref):
    tops, totals, top = read_stats(parts_ref)
    total, numer = merge(parts_ref, tops, totals, top)
    numer = numer.astype(BF16)
    stats = packed(top, total)
    for i in range(out_ref.shape[0]):
        out_ref[i, 0:DH, :] = numer
        out_ref[i, DH:, :] = stats


def finish_kernel(parts_ref, q_ref, new_ref, positions_ref, out_ref):
    place = lax.axis_index("near")
    qcount = q_ref.shape[0]
    groups = DH // qcount
    head = pl.multiple_of(place * groups // GROUPS * DH, DH)
    q = [
        q_ref[:, pl.ds(pl.multiple_of((place * groups + s) * DH, DH), DH)] for s in range(groups)
    ]
    q = jnp.concatenate(q, axis=0)
    new_keys = new_ref[0, :, pl.ds(head, DH)]
    new_values = new_ref[1, :, pl.ds(head, DH)]
    scores = lax.dot_general(q, new_keys, NT, preferred_element_type=F32) * TO_LOG2
    token = lax.broadcasted_iota(jnp.int32, scores.shape, 0) % qcount
    own = token == lax.broadcasted_iota(jnp.int32, scores.shape, 1)
    positions = jnp.broadcast_to(positions_ref[...], scores.shape)
    own_position = jnp.max(jnp.where(own, positions, -1), axis=1, keepdims=True)
    visible = positions <= own_position
    scores = jnp.where(visible, scores, HIDDEN)
    new_top = jnp.max(scores, axis=1, keepdims=True)
    on_diagonal = diagonal()

    def along_lanes(column):
        spread = jnp.where(on_diagonal, jnp.broadcast_to(column, (DH, DH)), 0.0)
        return jnp.sum(spread, axis=0, keepdims=True)

    def along_rows(row):
        spread = jnp.where(on_diagonal, jnp.broadcast_to(row, (DH, DH)), 0.0)
        return jnp.sum(spread, axis=1, keepdims=True)

    tops, totals, top = read_stats(parts_ref)
    top = jnp.maximum(top, along_lanes(new_top))
    total, numer = merge(parts_ref, tops, totals, top)
    weights = jnp.exp2(scores - along_rows(top))
    numer = numer + lax.dot_general(
        weights.astype(BF16), new_values, NN, preferred_element_type=F32
    )
    total = along_rows(total) + jnp.sum(weights, axis=1, keepdims=True)
    attended = (numer / total).astype(BF16)
    for i in range(out_ref.shape[0]):
        out_ref[i] = attended


def project_kernel(parts_ref, weight_ref, out_ref, left_ref):
    qcount = left_ref.shape[0]
    groups = DH // qcount
    for i in range(parts_ref.shape[0]):
        for s in range(groups):
            col = (i * groups + s) * DH
            left_ref[:, col : col + DH] = parts_ref[i, s * qcount : (s + 1) * qcount, :]
    out_ref[...] = lax.dot_general(
        left_ref[...], weight_ref[...], NN, preferred_element_type=F32
    ).astype(BF16)


def per_device(queries, cache_k, cache_v, kv_scale, new_kv, fill_lengths, positions, out_weight):
    qcount, width = queries.shape
    slots = cache_k.shape[0]
    heads = cache_k.shape[1] // DH
    near, far = lax.axis_size("near"), lax.axis_size("far")
    tile_len = 2048
    smem = pl.BlockSpec(memory_space=pltpu.SMEM)
    vmem = pl.BlockSpec(memory_space=pltpu.VMEM)
    hbm = pl.BlockSpec(memory_space=pltpu.HBM)
    params = pltpu.CompilerParams(vmem_limit_bytes=48 * 1024 * 1024)

    def in_hbm(x):
        return pltpu.with_memory_space_constraint(x, pltpu.HBM)

    parts = pl.pallas_call(
        functools.partial(attend_kernel, tile_len),
        in_specs=[hbm, hbm, hbm, hbm, smem],
        out_specs=vmem,
        out_shape=jax.ShapeDtypeStruct((near, DH + STATS, DH), BF16),
        scratch_shapes=attend_scratch(qcount, width, slots, heads, tile_len),
        compiler_params=params,
        name="attend",
    )(
        in_hbm(queries),
        in_hbm(cache_k),
        in_hbm(cache_v),
        in_hbm(kv_scale.transpose(0, 2, 1)),
        fill_lengths,
    )

    parts = lax.all_to_all(parts, "near", 0, 0)
    parts = pl.pallas_call(
        merge_kernel,
        in_specs=[vmem],
        out_specs=vmem,
        out_shape=jax.ShapeDtypeStruct((far, DH + STATS, DH), BF16),
        compiler_params=params,
        name="merge",
    )(parts)
    parts = lax.all_to_all(parts, "far", 0, 0)

    attended = pl.pallas_call(
        finish_kernel,
        in_specs=[vmem, vmem, vmem, vmem],
        out_specs=vmem,
        out_shape=jax.ShapeDtypeStruct((near, DH, DH), BF16),
        compiler_params=params,
        name="finish",
    )(
        parts,
        queries,
        new_kv,
        positions.reshape(1, qcount),
    )
    attended = lax.all_to_all(attended, "near", 0, 0)

    share = pl.pallas_call(
        project_kernel,
        in_specs=[vmem, vmem],
        out_specs=vmem,
        out_shape=jax.ShapeDtypeStruct((qcount, out_weight.shape[1]), BF16),
        scratch_shapes=[pltpu.VMEM((qcount, width), BF16)],
        compiler_params=params,
        name="project",
    )(attended, out_weight)

    n = lax.axis_size("kv")
    total = share.astype(F32)
    for shift in range(1, n):
        other = lax.ppermute(share, "kv", [(i, (i + shift) % n) for i in range(n)])
        total = total + other.astype(F32)
    return total.astype(BF16)


def solution(mesh):
    ctx, kv = mesh.devices.shape
    mesh = Mesh(mesh.devices.reshape(ctx // NEAR, NEAR, kv), ("far", "near", "kv"))
    ctx = ("far", "near")
    placed = (
        P(None, "kv"),
        P(ctx, "kv"),
        P(ctx, "kv"),
        P(None, ctx, "kv"),
        P(None, None, "kv"),
        P(ctx),
        P(),
        P("kv", ctx),
    )
    return jax.shard_map(
        per_device, mesh=mesh, in_specs=placed, out_specs=P(None, ctx), check_vma=False
    )
```
